32 devices in a mesh: req: 8 (over z, y), mlp: 4 (over x, core).
Axes of the slice: x: 2, y: 2, z: 4, core: 2. Of those that a mesh axis runs over, the one named last changes fastest.
Arguments:
- hidden: bfloat16 [4096, 3584], P('req', 'mlp'), may hold values from -6 to 6
- query_heads: bfloat16 [4096, 3584], P('req', 'mlp'), may hold values from -4 to 4
- key_heads: bfloat16 [4096, 3584], P('req', 'mlp'), may hold values from -4 to 4
- value_heads: bfloat16 [4096, 3584], P('req', 'mlp'), may hold values from -6 to 6
- segment_ids: int32 [4096], P('req'), may hold values from 0 to 31, never falling along the last dimension, each value on 1 to 1024 neighbouring positions
- page_table: int32 [8, 32], P('req'), may hold values from 0 to 31, each once within a row
- mamba_conv_input: bfloat16 [4096, 7168], P('req', 'mlp'), may hold values from -6 to 6
- mamba_output_gate: bfloat16 [4096, 7168], P('req', 'mlp'), may hold values from -6 to 6
- state_input_projection: bfloat16 [4096, 128], P('req'), may hold values from -6 to 6
- state_output_projection: bfloat16 [4096, 128], P('req'), may hold values from -6 to 6
- discrete_step_size: float32 [4096, 112], P('req', 'mlp'), may hold values from 0.24 to 100, as said below
- head_decay_rate: float32 [112], P('mlp'), may hold values from 0.00024414062 to 0.05, as said below
- skip_gain: float32 [112], P('mlp'), may hold values from 0.5 to 2
- mamba_gated_norm_gain: float32 [7168], P('mlp'), may hold values from 0.1 to 1.9
- attn_proj: bfloat16 [3584, 3584], P('mlp'), may hold values from -0.09375 to 0.09375
- mamba_output_projection: bfloat16 [7168, 3584], P('mlp'), may hold values from -0.0625 to 0.0625
- mlp_norm_gain: float32 [3584], replicated, may hold values from 0.1 to 1.9
- gate_proj: bfloat16 [3584, 7168], P('req', 'mlp'), may hold values from -0.09375 to 0.09375
- up_proj: bfloat16 [3584, 7168], P('req', 'mlp'), may hold values from -0.09375 to 0.09375
- down_proj: bfloat16 [7168, 3584], P('mlp', 'req'), may hold values from -0.0625 to 0.0625
- next_norm_gain: float32 [3584], P('mlp'), may hold values from 0.1 to 1.9
Outputs:
- new_hidden: bfloat16 [4096, 3584], P('req', 'mlp')
- next_normed: bfloat16 [4096, 3584], P('req', 'mlp')
- kv_cache: bfloat16 [2, 16, 256, 3584], P(None, 'mlp', 'req')
The draws below stay inside these ranges and needn't reach their ends.
Inputs may be any that keep to these rules, and one draw needn't show every extreme that they name: `segment_ids`: prompt ids never fall along the stream; a prompt has 1 to 1024 tokens and one has exactly 1024. `page_table`: each request group's row names every page of its pool once. `discrete_step_size`: Positive. `head_decay_rate`: Positive.
All inputs are finite; a program needn't handle non-finite values.
Results may differ from the reference program's by a relative error of at most 0.006.
Values may be sent and summed in bfloat16 or wider, within the bound.
A program may use at most 192 MiB of HBM per device.

```python
import math
import jax
import jax.numpy as jnp
import numpy as np
from jax import lax

MODEL_WIDTH = 3584
HEADS_A = 16
HD = 224
MAMBA_HEAD_COUNT = 112
MAMBA_HEAD_SIZE = 64
STATE_SIZE = 64
STATE_GROUPS = 2
FF = 7168
PROMPT_SPAN = 512
REACH = 2
PAGE = 16
PACKED_LENGTH = 4096
MAXLEN = 1024
NSEG = 32
PAGES_DEV = 32
N_REQ = 8


def query_key_pair(master_seed_draw):
    first_key = jax.random.fold_in(master_seed_draw, 11)
    second_key = jax.random.fold_in(master_seed_draw, 12)
    array_shape = (PACKED_LENGTH, HEADS_A * HD)
    queries = jnp.clip(jax.random.normal(first_key, array_shape, jnp.float32), -4.0, 4.0)
    keys_drawn = jnp.clip(jax.random.normal(second_key, array_shape, jnp.float32), -4.0, 4.0)
    return (queries, keys_drawn)


def draw_query_heads(master_seed_draw, part):
    return query_key_pair(master_seed_draw)[0].astype(jnp.bfloat16)


def draw_key_heads(master_seed_draw, part):
    return query_key_pair(master_seed_draw)[1].astype(jnp.bfloat16)


def draw_discrete_step_size(master_seed_draw, part):
    level_key = jax.random.fold_in(master_seed_draw, 21)
    block_key = jax.random.fold_in(master_seed_draw, 22)
    flurry_seed_draw = jax.random.fold_in(master_seed_draw, 23)
    levels = jnp.exp(jax.random.uniform(level_key, (PACKED_LENGTH, MAMBA_HEAD_COUNT), jnp.float32, -0.7, 0.7))
    block_scale = jnp.exp(jax.random.uniform(block_key, (PACKED_LENGTH // PROMPT_SPAN, 1), jnp.float32, -0.7, 0.7))
    rescaled_amounts = (levels.reshape(PACKED_LENGTH // PROMPT_SPAN, PROMPT_SPAN, MAMBA_HEAD_COUNT) * block_scale[:, :, None]).reshape(PACKED_LENGTH, MAMBA_HEAD_COUNT)
    flurry_spans = jax.random.randint(flurry_seed_draw, (PACKED_LENGTH, 1), 0, PROMPT_SPAN) < 2
    return jnp.where(flurry_spans, 100.0, rescaled_amounts).astype(jnp.float32)


def draw_head_decay_rate(master_seed_draw, part):
    slow_key = jax.random.fold_in(master_seed_draw, 31)
    lowest = math.log(0.25 / MAXLEN)
    highest = math.log(0.05)
    return jnp.exp(jax.random.uniform(slow_key, (MAMBA_HEAD_COUNT,), jnp.float32, lowest, highest)).astype(jnp.float32)


def steps_of(rng, dims, cuts, low, largest):
    factor_of, own = 1.0, jax.random.fold_in(rng, 6)
    for axis_at, blocks in cuts:
        heights = jnp.exp(jax.random.uniform(jax.random.fold_in(own, axis_at), (blocks,), jnp.float32, low / len(cuts), largest / len(cuts)))
        factor_of = factor_of * jnp.repeat(heights, dims[axis_at] // blocks).reshape([-1 if axis == axis_at else 1 for axis in range(len(dims))])
    return factor_of


def length_profile(amount, total, limit, slope):
    weights = [(1 << 20) // math.isqrt(grade ** slope) + 1 for grade in range(2, amount + 1)]
    surplus, holding = total - limit - (amount - 1), [1] * (amount - 1)
    while surplus > 0:
        movable = [i for i in range(amount - 1) if holding[i] < limit]
        pool, budget = sum([weights[i] for i in movable]), surplus
        for i in movable:
            addition = min(limit - holding[i], max(1, budget * weights[i] // pool), surplus)
            holding[i] = holding[i] + addition
            surplus = surplus - addition
    return np.array([limit] + holding)


def ragged_sizes(key, number_of, total, most, lean):
    if number_of == 2:
        one = jax.random.randint(key, (), max(1, total - most), min(most, total - 1) + 1)
        return jnp.stack([one, total - one])
    tallies = jnp.asarray(length_profile(number_of, total, most, lean), jnp.int32)
    couples = (number_of - 1) // 2
    source_of, receiver = tallies[1:1 + 2 * couples:2], tallies[2:2 + 2 * couples:2]
    margin = jnp.minimum(source_of - 1, most - receiver)
    moved = jax.random.randint(jax.random.fold_in(key, 1), (couples,), 0, 1 << 20) % (margin + 1)
    tallies = tallies.at[1:1 + 2 * couples:2].set(source_of - moved).at[2:2 + 2 * couples:2].set(receiver + moved)
    return tallies[jax.random.permutation(jax.random.fold_in(key, 2), number_of)]


def centred(own_key, shape, scale, most, split=(), kind=jnp.bfloat16):
    entries = jax.random.normal(own_key, shape, jnp.float32) * scale
    if len(split) > 0:
        entries = steps_of(own_key, shape, split, -0.22, 0.18) * entries
    return jnp.clip(entries, min=-most, max=most).astype(kind)


def setup_inputs(seed: int = 0) -> dict:
    streams_of = jax.random.split(jax.random.key(seed), 22)
    hidden = centred(streams_of[0], (PACKED_LENGTH, MODEL_WIDTH), 1.0, 6.0, ((0, 8), (1, 4)))
    query_heads = draw_query_heads(jax.random.fold_in(streams_of[21], 71), 0)
    key_heads = draw_key_heads(jax.random.fold_in(streams_of[21], 71), 0)
    value_heads = centred(streams_of[3], (PACKED_LENGTH, HEADS_A * HD), 1.0, 6.0, ((0, 8), (1, 4)))
    segment_ids = jnp.searchsorted(jnp.cumsum(ragged_sizes(streams_of[4], NSEG, PACKED_LENGTH, MAXLEN, 3)), jnp.arange(PACKED_LENGTH), side="right").astype(jnp.int32)
    page_table = jax.vmap(lambda own: jax.random.permutation(own, PAGES_DEV))(jax.random.split(streams_of[5], N_REQ)).reshape((N_REQ, PAGES_DEV)).astype(jnp.int32)
    mamba_conv_input = centred(streams_of[6], (PACKED_LENGTH, MAMBA_HEAD_COUNT * MAMBA_HEAD_SIZE), 1.0, 6.0, ((0, 8), (1, 4)))
    mamba_output_gate = centred(streams_of[7], (PACKED_LENGTH, MAMBA_HEAD_COUNT * MAMBA_HEAD_SIZE), 1.0, 6.0, ((0, 8), (1, 4)))
    state_input_projection = centred(streams_of[8], (PACKED_LENGTH, STATE_GROUPS * STATE_SIZE), 1.0, 6.0, ((0, 8),))
    state_output_projection = centred(streams_of[9], (PACKED_LENGTH, STATE_GROUPS * STATE_SIZE), 1.0, 6.0, ((0, 8),))
    discrete_step_size = draw_discrete_step_size(jax.random.fold_in(streams_of[21], 71), 0)
    head_decay_rate = draw_head_decay_rate(jax.random.fold_in(streams_of[21], 71), 0)
    skip_gain = jnp.clip(0.5 + 1.5 * jax.random.uniform(streams_of[12], (MAMBA_HEAD_COUNT,), jnp.float32) ** steps_of(streams_of[12], (MAMBA_HEAD_COUNT,), ((0, 4),), -0.2, 0.2), 0.5, 2.0)
    mamba_gated_norm_gain = jnp.clip(1.0 + 0.18 * jax.random.normal(streams_of[13], (MAMBA_HEAD_COUNT * MAMBA_HEAD_SIZE,), jnp.float32), 0.1, 1.9)
    attn_proj = centred(streams_of[14], (HEADS_A * HD, MODEL_WIDTH), (HEADS_A * HD) ** -0.5, 0.09375, ((0, 4),))
    mamba_output_projection = centred(streams_of[15], (MAMBA_HEAD_COUNT * MAMBA_HEAD_SIZE, MODEL_WIDTH), (MAMBA_HEAD_COUNT * MAMBA_HEAD_SIZE) ** -0.5, 0.0625, ((0, 4),))
    mlp_norm_gain = jnp.clip(1.0 + 0.18 * jax.random.normal(streams_of[16], (MODEL_WIDTH,), jnp.float32), 0.1, 1.9)
    gate_proj = centred(streams_of[17], (MODEL_WIDTH, FF), MODEL_WIDTH ** -0.5, 0.09375, ((0, 8), (1, 4)))
    up_proj = centred(streams_of[18], (MODEL_WIDTH, FF), MODEL_WIDTH ** -0.5, 0.09375, ((0, 8), (1, 4)))
    down_proj = centred(streams_of[19], (FF, MODEL_WIDTH), FF ** -0.5, 0.0625, ((0, 4), (1, 8)))
    next_norm_gain = jnp.clip(1.0 + 0.18 * jax.random.normal(streams_of[20], (MODEL_WIDTH,), jnp.float32), 0.1, 1.9)
    return {"hidden": hidden, "query_heads": query_heads, "key_heads": key_heads, "value_heads": value_heads, "segment_ids": segment_ids, "page_table": page_table, "mamba_conv_input": mamba_conv_input, "mamba_output_gate": mamba_output_gate, "state_input_projection": state_input_projection, "state_output_projection": state_output_projection, "discrete_step_size": discrete_step_size, "head_decay_rate": head_decay_rate, "skip_gain": skip_gain, "mamba_gated_norm_gain": mamba_gated_norm_gain, "attn_proj": attn_proj, "mamba_output_projection": mamba_output_projection, "mlp_norm_gain": mlp_norm_gain, "gate_proj": gate_proj, "up_proj": up_proj, "down_proj": down_proj, "next_norm_gain": next_norm_gain}


EPSILON = 1e-05
exact_mode = lax.Precision.HIGHEST

def attend_rows(query_rows, segment_rows, pos_rows, key_block, value_block, key_segs, key_pos, head_count):
    row_total = query_rows.shape[0]
    key_total = key_block.shape[0]
    query_float = query_rows.astype(jnp.float32).reshape(row_total, head_count, HD)
    key_float = key_block.astype(jnp.float32).reshape(key_total, head_count, HD)
    value_float = value_block.astype(jnp.float32).reshape(key_total, head_count, HD)
    scores = jnp.einsum('qhd,khd->hqk', query_float, key_float) * (1.0 / math.sqrt(HD))
    allowed = (segment_rows[:, None] == key_segs[None, :]) & (key_pos[None, :] <= pos_rows[:, None])
    scores = jnp.where(allowed[None, :, :], scores, -jnp.inf)
    top_score = lax.optimization_barrier(jnp.max(scores, axis=2, keepdims=True))
    raised = jnp.exp(scores - top_score)
    weights = (raised / lax.optimization_barrier(jnp.sum(raised, axis=2, keepdims=True))).astype(jnp.bfloat16)
    summed = jnp.einsum('hqk,khd->qhd', weights.astype(jnp.float32), value_float)
    return summed.astype(jnp.bfloat16).reshape(row_total, head_count * HD)

def block_contributions(input_token_rows, input_proj_rows, output_proj_rows, step_size_rows, head_decay_rate, segment_rows, segment_prior_state, group_index, head_width):
    row_count = input_token_rows.shape[0]
    head_count = step_size_rows.shape[1]
    input_float = input_token_rows.astype(jnp.float32).reshape(row_count, head_count, head_width)
    b_float = input_proj_rows.astype(jnp.float32)
    c_float = output_proj_rows.astype(jnp.float32)
    running = jnp.cumsum(-step_size_rows * head_decay_rate[None, :], axis=0)
    positions = jnp.arange(row_count, dtype=jnp.int32)
    live = (segment_rows[:, None] == segment_rows[None, :]) & (positions[:, None] >= positions[None, :])
    spread = running.T[:, :, None] - running.T[:, None, :]
    mixing = jnp.exp(jnp.where(live[None, :, :], spread, -1e+30))
    inner = jnp.einsum('tgn,ugn->gtu', c_float, b_float, precision=exact_mode)
    driven = input_float * step_size_rows[:, :, None]
    local_output = jnp.einsum('htu,uhp->thp', mixing * inner[group_index], driven, precision=exact_mode)
    b_per_head = b_float[:, group_index, :]
    output_proj_per_head = c_float[:, group_index, :]
    tail_rows = segment_rows == segment_rows[row_count - 1]
    tail_gain = jnp.where(tail_rows[:, None], jnp.exp(running[row_count - 1][None, :] - running), 0.0)
    state_local_part = jnp.einsum('uh,uhp,uhn->hpn', tail_gain, driven, b_per_head, precision=exact_mode)
    decay_cumulative = jnp.where(segment_rows[row_count - 1] == segment_prior_state, jnp.exp(running[row_count - 1]), 0.0)
    entry_weighting = jnp.where((segment_rows == segment_prior_state)[:, None], jnp.exp(running), 0.0)
    return (local_output, decay_cumulative, state_local_part, entry_weighting, input_float, output_proj_per_head)

def finish(local_output, entry_weighting, input_float, output_proj_per_head, carry_in, skip_gain):
    carried = jnp.einsum('hpn,thn->thp', carry_in, output_proj_per_head, precision=exact_mode)
    result = local_output + entry_weighting[:, :, None] * carried + skip_gain[None, :, None] * input_float
    return result.reshape(result.shape[0], result.shape[1] * result.shape[2])

def reference(hidden, query_heads, key_heads, value_heads, segment_ids, page_table, mamba_conv_input, mamba_output_gate, state_input_projection, state_output_projection, discrete_step_size, head_decay_rate, skip_gain, mamba_gated_norm_gain, attn_proj, mamba_output_projection, mlp_norm_gain, gate_proj, up_proj, down_proj, next_norm_gain):
    lead_rows = REACH * PROMPT_SPAN
    feature_count = HEADS_A * HD
    key_padded = jnp.concatenate([jnp.zeros((lead_rows, feature_count), key_heads.dtype), key_heads], axis=0)
    value_padded = jnp.concatenate([jnp.zeros((lead_rows, feature_count), value_heads.dtype), value_heads], axis=0)
    seg_padded = jnp.concatenate([jnp.full((lead_rows,), -2, jnp.int32), segment_ids.astype(jnp.int32)])
    pos_padded = jnp.arange(PACKED_LENGTH + lead_rows, dtype=jnp.int32) - lead_rows

    def one_group(group_number):
        first_row = (group_number * PROMPT_SPAN).astype(jnp.int32)
        query_rows = lax.dynamic_slice_in_dim(query_heads, first_row, PROMPT_SPAN, 0)
        segment_rows = lax.dynamic_slice_in_dim(segment_ids, first_row, PROMPT_SPAN, 0)
        pos_rows = first_row + jnp.arange(PROMPT_SPAN, dtype=jnp.int32)
        key_block = lax.dynamic_slice_in_dim(key_padded, first_row, lead_rows + PROMPT_SPAN, 0)
        value_block = lax.dynamic_slice_in_dim(value_padded, first_row, lead_rows + PROMPT_SPAN, 0)
        key_segs = lax.dynamic_slice_in_dim(seg_padded, first_row, lead_rows + PROMPT_SPAN, 0)
        key_pos = lax.dynamic_slice_in_dim(pos_padded, first_row, lead_rows + PROMPT_SPAN, 0)
        return attend_rows(query_rows, segment_rows, pos_rows, key_block, value_block, key_segs, key_pos, HEADS_A)
    attended = lax.map(one_group, jnp.arange(N_REQ, dtype=jnp.int32)).reshape(PACKED_LENGTH, feature_count)
    page_total = N_REQ * PAGES_DEV

    def to_pages(source):
        return source.reshape(page_total, PAGE, HEADS_A, HD).transpose(2, 0, 1, 3).reshape(HEADS_A, page_total, PAGE * HD)
    target = (page_table.astype(jnp.int32) + PAGES_DEV * jnp.arange(N_REQ, dtype=jnp.int32)[:, None]).reshape(page_total)
    stacked = jnp.stack([to_pages(key_heads), to_pages(value_heads)])
    kv_cache = jnp.zeros_like(stacked).at[:, :, target].set(stacked)
    group_values = MAMBA_HEAD_COUNT // STATE_GROUPS
    head_group_index = (jnp.arange(MAMBA_HEAD_COUNT, dtype=jnp.int32) % STATE_GROUPS).astype(jnp.int32)
    segment_group_list = segment_ids.astype(jnp.int32).reshape(N_REQ, PROMPT_SPAN)
    segment_prior_state = jnp.concatenate([jnp.full((1,), -1, jnp.int32), segment_group_list[:-1, PROMPT_SPAN - 1]])
    sliced_values = (mamba_conv_input.reshape(N_REQ, PROMPT_SPAN, MAMBA_HEAD_COUNT * MAMBA_HEAD_SIZE), state_input_projection.reshape(N_REQ, PROMPT_SPAN, STATE_GROUPS, STATE_SIZE), state_output_projection.reshape(N_REQ, PROMPT_SPAN, STATE_GROUPS, STATE_SIZE), discrete_step_size.reshape(N_REQ, PROMPT_SPAN, MAMBA_HEAD_COUNT), segment_group_list, segment_prior_state)

    def advance_step(carried, pieces):
        input_token_rows, input_proj_rows, output_proj_rows, step_size_rows, segment_rows, prior_state = pieces
        local_output, decay_cumulative, state_local_part, entry_weighting, input_float, output_proj_per_head = block_contributions(input_token_rows, input_proj_rows, output_proj_rows, step_size_rows, head_decay_rate, segment_rows, prior_state, head_group_index, MAMBA_HEAD_SIZE)
        result = finish(local_output, entry_weighting, input_float, output_proj_per_head, carried, skip_gain)
        return (decay_cumulative[:, None, None] * carried + state_local_part, result)
    ignored_value, output_rows = lax.scan(advance_step, jnp.zeros((MAMBA_HEAD_COUNT, MAMBA_HEAD_SIZE, STATE_SIZE), jnp.float32), sliced_values)
    mamba_output = output_rows.reshape(PACKED_LENGTH, MAMBA_HEAD_COUNT * MAMBA_HEAD_SIZE)
    gated_output = mamba_output * jax.nn.silu(mamba_output_gate.astype(jnp.float32))
    grouped_values = gated_output.reshape(PACKED_LENGTH, MAMBA_HEAD_COUNT // STATE_GROUPS, STATE_GROUPS, MAMBA_HEAD_SIZE)
    group_mean = lax.optimization_barrier(jnp.sum(grouped_values * grouped_values, axis=(1, 3))) / (group_values * MAMBA_HEAD_SIZE)
    inverse_root_mean = lax.rsqrt(group_mean + EPSILON)
    mamba_normalized_rows = ((grouped_values * inverse_root_mean[:, None, :, None]).reshape(PACKED_LENGTH, MAMBA_HEAD_COUNT * MAMBA_HEAD_SIZE) * mamba_gated_norm_gain[None, :]).astype(jnp.bfloat16)
    mixed_rows = hidden.astype(jnp.float32) + jnp.dot(attended, attn_proj, preferred_element_type=jnp.float32) + jnp.dot(mamba_normalized_rows, mamba_output_projection, preferred_element_type=jnp.float32)
    normed = (mixed_rows * lax.rsqrt(lax.optimization_barrier(jnp.mean(mixed_rows * mixed_rows, axis=1, keepdims=True)) + EPSILON) * mlp_norm_gain[None, :]).astype(jnp.bfloat16)
    gate_act = jnp.dot(normed, gate_proj, preferred_element_type=jnp.float32)
    up_act = jnp.dot(normed, up_proj, preferred_element_type=jnp.float32)
    latent_activation = (jax.nn.silu(gate_act) * up_act).astype(jnp.bfloat16)
    new_hidden = (mixed_rows + jnp.dot(latent_activation, down_proj, preferred_element_type=jnp.float32)).astype(jnp.bfloat16)
    widened = new_hidden.astype(jnp.float32)
    next_normed = (widened * lax.rsqrt(lax.optimization_barrier(jnp.mean(widened * widened, axis=1, keepdims=True)) + EPSILON) * next_norm_gain[None, :]).astype(jnp.bfloat16)
    return (new_hidden, next_normed, kv_cache)
```

```python
import math

import jax
import jax.numpy as jnp
from jax import lax
from jax.experimental import pallas as pl
from jax.experimental.pallas import tpu as pltpu
from jax.sharding import PartitionSpec as P

HD = 224
MAMBA_HEAD_COUNT = 112
MAMBA_HEAD_SIZE = 64
STATE_SIZE = 64
STATE_GROUPS = 2
REACH = 2
PAGE = 16
LANES = 128
CHUNK = 128
QUERY_BLOCK = 128

EPSILON = 1e-05
exact_mode = lax.Precision.HIGHEST


def from_behind(value, axis, steps):
    count = lax.axis_size(axis)
    return lax.ppermute(value, axis, [(source, source + steps) for source in range(count - steps)])


def weight_blocks(gate_proj, up_proj, down_proj):
    count = lax.axis_size("req")
    me = lax.axis_index("req")
    line = 4
    cross = count // line

    def exchange(value, flip):
        return lax.ppermute(value, "req", [(source, source ^ flip) for source in range(count)])

    own = (gate_proj, up_proj, down_proj.T)
    held = [(0, own)]
    for step in range(1, line):
        flip = step * cross
        held.append((flip, tuple(exchange(part, flip) for part in own)))
    blocks = list(held)
    for flip, block in held:
        for step in range(1, cross):
            blocks.append((flip ^ step, tuple(exchange(part, step) for part in block)))
    return [(jnp.bitwise_xor(me, flip), block) for flip, block in blocks]


def attention_kernel(q_ref, k2, k1, k0, v2, v1, v0, seg_q, seg_k, out_ref):
    rows = q_ref.shape[0]
    span = k0.shape[0]
    width = q_ref.shape[1]
    first = REACH * span + pl.program_id(0) * rows
    pos_q = first + lax.broadcasted_iota(jnp.int32, (rows, 1), 0)
    pos_k = lax.broadcasted_iota(jnp.int32, (1, (REACH + 1) * span), 1)
    allowed = (seg_q[...] == seg_k[...]) & (pos_k <= pos_q)
    bias = jnp.where(allowed, 0.0, -1e30)
    keys = (k2, k1, k0)
    values = (v2, v1, v0)
    tiles = [None] * (-(-width // LANES))
    for head in range(width // HD):
        low, high = head * HD, (head + 1) * HD
        start, stop = low // LANES * LANES, min(-(-high // LANES) * LANES, width)
        lane = start + lax.broadcasted_iota(jnp.int32, (1, stop - start), 1)
        inside = (lane >= low) & (lane < high)
        query = jnp.where(inside, q_ref[:, start:stop], jnp.zeros((), q_ref.dtype))
        scores = jnp.concatenate(
            [
                lax.dot_general(
                    query,
                    key[:, start:stop],
                    (((1,), (1,)), ((), ())),
                    preferred_element_type=jnp.float32,
                )
                for key in keys
            ],
            axis=1,
        )
        scores = scores * (1.0 / math.sqrt(HD)) + bias
        raised = jnp.exp(scores - jnp.max(scores, axis=1, keepdims=True))
        total = jnp.sum(raised, axis=1, keepdims=True)
        weights = raised.astype(jnp.bfloat16)
        summed = sum(
            jnp.dot(
                weights[:, part * span : (part + 1) * span],
                value[:, start:stop],
                preferred_element_type=jnp.float32,
            )
            for part, value in enumerate(values)
        )
        summed = jnp.where(inside, summed / total, 0.0)
        for tile in range(start // LANES, -(-stop // LANES)):
            piece = summed[:, tile * LANES - start : min((tile + 1) * LANES, stop) - start]
            tiles[tile] = piece if tiles[tile] is None else tiles[tile] + piece
    for tile, piece in enumerate(tiles):
        out_ref[:, tile * LANES : tile * LANES + piece.shape[1]] = piece.astype(out_ref.dtype)


def attention(query_heads, keys, values, segment_ids, key_segs):
    rows, width = query_heads.shape
    whole = pl.BlockSpec((rows, width), lambda i: (0, 0))
    block = pl.BlockSpec((QUERY_BLOCK, width), lambda i: (i, 0))
    reached = (REACH + 1) * rows
    return pl.pallas_call(
        attention_kernel,
        grid=(rows // QUERY_BLOCK,),
        in_specs=[block]
        + [whole] * 6
        + [
            pl.BlockSpec((QUERY_BLOCK, 1), lambda i: (i, 0)),
            pl.BlockSpec((1, reached), lambda i: (0, 0)),
        ],
        out_specs=block,
        out_shape=jax.ShapeDtypeStruct((rows, width), jnp.bfloat16),
        compiler_params=pltpu.CompilerParams(vmem_limit_bytes=48 * 2**20),
        cost_estimate=pl.CostEstimate(
            flops=4 * rows * reached * width * 8,
            bytes_accessed=16 * rows * width,
            transcendentals=rows * reached * 4,
        ),
        name="attention",
    )(query_heads, *keys, *values, segment_ids[:, None], key_segs[None, :])


def expand_matrix(heads):
    lane = jnp.arange(heads * MAMBA_HEAD_SIZE, dtype=jnp.int32)
    return (lane[None, :] // MAMBA_HEAD_SIZE == jnp.arange(heads)[:, None]).astype(jnp.float32)


def exact_dot(a, b):
    return jnp.dot(a, b, precision=exact_mode, preferred_element_type=jnp.float32)


def mamba_kernel(
    x_ref,
    gate_ref,
    b_ref,
    c_ref,
    run_ref,
    run_t,
    dt_t,
    entry_ref,
    tail_ref,
    decay_ref,
    skip_ref,
    expand_ref,
    seg_c,
    seg_r,
    carry_ref,
    gated_ref,
    squares_ref,
    state,
):
    rows, width = x_ref.shape

    @pl.when(pl.program_id(0) == 0)
    def _():
        state[...] = carry_ref[...]

    t_at = lax.broadcasted_iota(jnp.int32, (rows, rows), 0)
    u_at = lax.broadcasted_iota(jnp.int32, (rows, rows), 1)
    live = (seg_c[...] == seg_r[...]) & (u_at <= t_at)
    first_half = lax.broadcasted_iota(jnp.int32, (1, LANES), 1) < STATE_SIZE
    none = jnp.zeros((), jnp.bfloat16)
    b = b_ref[...]
    c = c_ref[...]
    inner = []
    for part in (first_half, ~first_half):
        product = lax.dot_general(
            jnp.where(part, c, none), b, (((1,), (1,)), ((), ())), preferred_element_type=jnp.float32
        )
        inner.append(jnp.where(live, product, 0.0))
    old = state[...]
    carried = jnp.dot(c, old.astype(jnp.bfloat16), preferred_element_type=jnp.float32)
    entry = exact_dot(entry_ref[...], expand_ref[...])
    tail = exact_dot(tail_ref[...], expand_ref[...])
    x = x_ref[...]
    weighted = (x.astype(jnp.float32) * tail).astype(jnp.bfloat16)
    added = lax.dot_general(
        b, weighted, (((0,), (0,)), ((), ())), preferred_element_type=jnp.float32
    )
    row_half = lax.broadcasted_iota(jnp.int32, (LANES, LANES), 0) < STATE_SIZE
    lane_half = lax.broadcasted_iota(jnp.int32, (LANES, LANES), 1) < STATE_SIZE
    same = row_half == lane_half
    squares = jnp.zeros((rows, LANES), jnp.float32)
    for pair in range(width // LANES):
        at = slice(pair * LANES, (pair + 1) * LANES)
        x_pair = x[:, at]
        y = entry[:, at] * carried[:, at] + skip_ref[:, at] * x_pair.astype(jnp.float32)
        for half in range(2):
            head = 2 * pair + half
            spread = run_ref[:, head : head + 1] - run_t[head : head + 1, :]
            mixing = jnp.exp(jnp.minimum(spread, 0.0)) * dt_t[head : head + 1, :] * inner[half]
            part = first_half if half == 0 else ~first_half
            y = y + jnp.dot(
                mixing.astype(jnp.bfloat16),
                jnp.where(part, x_pair, none),
                preferred_element_type=jnp.float32,
            )
        gate = gate_ref[:, at].astype(jnp.float32)
        gated = y * (gate / (1.0 + jnp.exp(-gate)))
        gated_ref[:, at] = gated
        squares = squares + gated * gated
        state[:, at] = decay_ref[0, :, at] * old[:, at] + jnp.where(same, added[:, at], 0.0)
    squares_ref[:, 0:1] = jnp.sum(jnp.where(first_half, squares, 0.0), axis=1, keepdims=True)
    squares_ref[:, 1:2] = jnp.sum(jnp.where(first_half, 0.0, squares), axis=1, keepdims=True)


def mamba(x, gate, b, c, dt, rate, skip_gain, segment_ids, prior_segment):
    rows, width = x.shape
    heads = dt.shape[1]
    expand = expand_matrix(heads)
    running = jnp.cumsum(-dt * rate[None, :], axis=0)
    last_segment = segment_ids[rows - 1]
    tail_rows = segment_ids == last_segment
    tail = jnp.where(tail_rows[:, None], jnp.exp(running[rows - 1][None, :] - running), 0.0) * dt
    lane = jnp.arange(width, dtype=jnp.int32)
    state_row = jnp.arange(STATE_GROUPS * STATE_SIZE, dtype=jnp.int32)
    own = (state_row[:, None] // STATE_SIZE) == (lane[None, :] // MAMBA_HEAD_SIZE % STATE_GROUPS)
    weighted = (x.astype(jnp.float32) * exact_dot(tail, expand)).astype(jnp.bfloat16)
    ends = lax.dot_general(b, weighted, (((0,), (0,)), ((), ())), preferred_element_type=jnp.float32)
    ends = jnp.where(own, ends, 0.0)
    ends = ends[:STATE_SIZE] + ends[STATE_SIZE:]
    decay = jnp.where(last_segment == prior_segment, jnp.exp(running[rows - 1]), 0.0)
    decay = exact_dot(decay[None, :], expand)
    nearer = from_behind(jnp.concatenate([ends, decay], axis=0), "req", 1)
    farther = from_behind(ends, "req", 2)
    carry = nearer[:STATE_SIZE] + nearer[STATE_SIZE:] * farther
    carry = jnp.where(own, jnp.concatenate([carry, carry], axis=0), 0.0)

    chunks = rows // CHUNK
    run_chunks = running.reshape(chunks, CHUNK, heads)
    seg_chunks = segment_ids.reshape(chunks, CHUNK)
    run_end = run_chunks[:, CHUNK - 1]
    seg_end = seg_chunks[:, CHUNK - 1]
    run_before = jnp.concatenate([jnp.zeros_like(run_end[:1]), run_end[:-1]], axis=0)
    seg_before = jnp.concatenate([prior_segment[None], seg_end[:-1]], axis=0)
    entry = jnp.where(
        (seg_chunks == seg_before[:, None])[:, :, None],
        jnp.exp(run_chunks - run_before[:, None]),
        0.0,
    ).reshape(rows, heads)
    chunk_tail = jnp.where(
        (seg_chunks == seg_end[:, None])[:, :, None], jnp.exp(run_end[:, None] - run_chunks), 0.0
    ).reshape(rows, heads) * dt
    chunk_decay = jnp.where((seg_end == seg_before)[:, None], jnp.exp(run_end - run_before), 0.0)
    chunk_decay = exact_dot(chunk_decay, expand)[:, None, :]
    skip = exact_dot(skip_gain[None, :], expand)

    def by_row(columns):
        return pl.BlockSpec((CHUNK, columns), lambda i: (i, 0))

    def by_lane(count):
        return pl.BlockSpec((count, CHUNK), lambda i: (0, i))

    def whole(shape):
        return pl.BlockSpec(shape, lambda i: (0, 0))

    return pl.pallas_call(
        mamba_kernel,
        grid=(chunks,),
        in_specs=[
            by_row(width),
            by_row(width),
            by_row(LANES),
            by_row(LANES),
            by_row(heads),
            by_lane(heads),
            by_lane(heads),
            by_row(heads),
            by_row(heads),
            pl.BlockSpec((1, 1, width), lambda i: (i, 0, 0)),
            whole((1, width)),
            whole((heads, width)),
            by_row(1),
            by_lane(1),
            whole((LANES, width)),
        ],
        out_specs=[by_row(width), by_row(STATE_GROUPS)],
        out_shape=[
            jax.ShapeDtypeStruct((rows, width), jnp.float32),
            jax.ShapeDtypeStruct((rows, STATE_GROUPS), jnp.float32),
        ],
        scratch_shapes=[pltpu.VMEM((LANES, width), jnp.float32)],
        compiler_params=pltpu.CompilerParams(vmem_limit_bytes=48 * 2**20),
        cost_estimate=pl.CostEstimate(
            flops=rows * width * 4000, bytes_accessed=rows * width * 10, transcendentals=rows * width * 2
        ),
        name="mamba",
    )(
        x,
        gate,
        b,
        c,
        running,
        running.T,
        dt.T,
        entry,
        chunk_tail,
        chunk_decay,
        skip,
        expand,
        segment_ids[:, None],
        segment_ids[None, :],
        carry,
    )


def body(
    hidden,
    query_heads,
    key_heads,
    value_heads,
    segment_ids,
    page_table,
    mamba_conv_input,
    mamba_output_gate,
    state_input_projection,
    state_output_projection,
    discrete_step_size,
    head_decay_rate,
    skip_gain,
    mamba_gated_norm_gain,
    attn_proj,
    mamba_output_projection,
    mlp_norm_gain,
    gate_proj,
    up_proj,
    down_proj,
    next_norm_gain,
):
    row_count, lane_count = hidden.shape
    head_count = query_heads.shape[1] // HD
    width_total = attn_proj.shape[1]
    mamba_width = mamba_conv_input.shape[1]
    column = lax.axis_index("mlp")

    segment_parts = []
    key_parts = []
    value_parts = []
    for distance in range(REACH, 0, -1):
        segment_parts.append(from_behind(segment_ids + 1, "req", distance) - 1)
        key_parts.append(from_behind(key_heads, "req", distance))
        value_parts.append(from_behind(value_heads, "req", distance))
    key_segs = jnp.concatenate(segment_parts + [segment_ids], axis=0)
    prior_segment = segment_parts[-1][row_count - 1]

    blocks = weight_blocks(gate_proj, up_proj, down_proj)

    gated, squares = mamba(
        mamba_conv_input,
        mamba_output_gate,
        state_input_projection,
        state_output_projection,
        discrete_step_size,
        head_decay_rate,
        skip_gain,
        segment_ids,
        prior_segment,
    )
    totals = lax.psum(squares, "mlp")
    attended = attention(
        query_heads, key_parts + [key_heads], value_parts + [value_heads], segment_ids, key_segs
    )

    page_count = page_table.shape[1]
    pages = jnp.arange(page_count, dtype=jnp.int32)
    source_page = jnp.sum(
        jnp.where(page_table[0][None, :] == pages[:, None], pages[None, :], 0), axis=1
    )

    def cache_of(heads):
        ordered = heads.reshape(page_count, PAGE, head_count * HD)[source_page]
        return (
            ordered.reshape(page_count, PAGE, head_count, HD)
            .transpose(2, 0, 1, 3)
            .reshape(head_count, page_count, PAGE * HD)
        )

    kv_cache = jnp.stack([cache_of(key_heads), cache_of(value_heads)])

    inverse_group = lax.rsqrt(totals / (MAMBA_HEAD_COUNT // STATE_GROUPS * MAMBA_HEAD_SIZE) + EPSILON)
    first_group = jnp.arange(mamba_width, dtype=jnp.int32) // MAMBA_HEAD_SIZE % STATE_GROUPS == 0
    scale = jnp.where(first_group[None, :], inverse_group[:, 0:1], inverse_group[:, 1:2])
    mnormed = (gated * scale * mamba_gated_norm_gain[None, :]).astype(jnp.bfloat16)
    projected = jnp.dot(attended, attn_proj, preferred_element_type=jnp.float32) + jnp.dot(
        mnormed, mamba_output_projection, preferred_element_type=jnp.float32
    )
    mixed = lax.psum_scatter(
        projected, "mlp", scatter_dimension=1, tiled=True
    ) + hidden.astype(jnp.float32)
    mixed_squares = lax.psum(jnp.sum(mixed * mixed, axis=1), "mlp")
    own_gain = lax.dynamic_slice_in_dim(mlp_norm_gain, column * lane_count, lane_count)
    scaled = (mixed * own_gain[None, :]).astype(jnp.bfloat16)
    rows_all = lax.all_gather(scaled, "mlp", axis=1, tiled=True)
    inverse = lax.rsqrt(mixed_squares / width_total + EPSILON)[:, None]
    depth = gate_proj.shape[0]
    gate_sum = None
    up_sum = None
    for owner, block in blocks:
        part = lax.dynamic_slice_in_dim(rows_all, owner * depth, depth, 1)
        gate_part = jnp.dot(part, block[0], preferred_element_type=jnp.float32)
        up_part = jnp.dot(part, block[1], preferred_element_type=jnp.float32)
        gate_sum = gate_part if gate_sum is None else gate_sum + gate_part
        up_sum = up_part if up_sum is None else up_sum + up_part
    latent = (jax.nn.silu(gate_sum * inverse) * (up_sum * inverse)).astype(jnp.bfloat16)
    down_all = jnp.zeros((width_total, latent.shape[1]), jnp.bfloat16)
    for owner, block in blocks:
        down_all = lax.dynamic_update_slice_in_dim(down_all, block[2], owner * depth, 0)
    partial_value = lax.dot_general(
        latent, down_all, (((1,), (1,)), ((), ())), preferred_element_type=jnp.float32
    )
    mlp_share = lax.psum_scatter(
        partial_value.astype(jnp.bfloat16), "mlp", scatter_dimension=1, tiled=True
    )
    new_hidden = (mixed + mlp_share.astype(jnp.float32)).astype(jnp.bfloat16)
    widened = new_hidden.astype(jnp.float32)
    total_sq = lax.psum(jnp.sum(widened * widened, axis=1), "mlp")
    next_normed = (
        widened * lax.rsqrt(total_sq / width_total + EPSILON)[:, None] * next_norm_gain[None, :]
    ).astype(jnp.bfloat16)
    return (new_hidden, next_normed, kv_cache)


def solution(mesh):
    return jax.shard_map(
        body,
        mesh=mesh,
        in_specs=(
            P("req", "mlp"),
            P("req", "mlp"),
            P("req", "mlp"),
            P("req", "mlp"),
            P("req"),
            P("req", None),
            P("req", "mlp"),
            P("req", "mlp"),
            P("req", None),
            P("req", None),
            P("req", "mlp"),
            P("mlp"),
            P("mlp"),
            P("mlp"),
            P("mlp", None),
            P("mlp", None),
            P(),
            P("req", "mlp"),
            P("req", "mlp"),
            P("mlp", "req"),
            P("mlp"),
        ),
        out_specs=(P("req", "mlp"), P("req", "mlp"), P(None, "mlp", "req", None)),
        check_vma=False,
    )
```
